32 devices in a mesh: lrow: 2 (over x), rcol: 4 (over y, core), term: 4 (over z).
Axes of the slice: x: 2, y: 2, z: 4, core: 2. Of those that a mesh axis runs over, the one named last changes fastest.
Arguments:
- core_left: bfloat16 [256, 256, 128], P(None, 'rcol'), may hold values from -6 to 6
- core_right: bfloat16 [256, 256, 128], P('rcol', 'lrow'), may hold values from -0.03125 to 0.03125
- env_left: bfloat16 [20, 8, 256], P('term', 'lrow'), may hold values from -0.375 to 0.375
- env_right: bfloat16 [20, 256, 256], P('term'), may hold values from -0.375 to 0.375
- coef_left: float32 [20, 3, 128], P('term'), may hold values from -1.5 to 1.5
- coef_right: float32 [20, 3, 128], P('term'), may hold values from -1.5 to 1.5
- projected: bfloat16 [128, 8, 256, 128], P('term', 'lrow', 'rcol'), may hold values from -6 to 6
Outputs:
- residual: bfloat16 [128, 8, 256, 128], P('term', 'lrow', 'rcol')
The draws below stay inside these ranges and needn't reach their ends.
All inputs are finite; a program needn't handle non-finite values.
Results may differ from the reference program's by a relative error of at most 0.012.
Values may be sent and summed in bfloat16 or wider, within the bound.
A program may use at most 128 MiB of HBM per device.

```python
import jax
import jax.numpy as jnp
from jax import lax

RANK = 256
N = 128
TERMS = 20
SLAB = 8


def block_scale(rng, dims, split, least, high):
    loudness, own = 1.0, jax.random.fold_in(rng, 6)
    for axis_at, parts in split:
        draws = jnp.exp(jax.random.uniform(jax.random.fold_in(own, axis_at), (parts,), jnp.float32, least / len(split), high / len(split)))
        loudness = loudness * jnp.repeat(draws, dims[axis_at] // parts).reshape([-1 if axis == axis_at else 1 for axis in range(len(dims))])
    return loudness


def gaussian(rng, dims, spread, bound, pieces=(), dtype=jnp.bfloat16):
    factor_of = block_scale(rng, dims, pieces, -0.22, 0.18) if pieces else 1.0
    drawn = jax.random.normal(rng, dims, jnp.float32) * spread * factor_of
    return jnp.minimum(jnp.maximum(drawn, -bound), bound).astype(dtype)


def setup_inputs(seed: int = 0) -> dict:
    keys = jax.random.split(jax.random.key(seed), 8)
    core_left = gaussian(keys[0], (RANK, RANK, N), 1.0, 6.0, ((1, 4),))
    core_right = gaussian(keys[1], (RANK, RANK, N), (8 * TERMS * RANK) ** -0.5, 0.03125, ((0, 4), (1, 2)))
    env_left = gaussian(keys[2], (TERMS, SLAB, RANK), RANK ** -0.5, 0.375, ((0, 4), (1, 2)))
    env_right = gaussian(keys[3], (TERMS, RANK, RANK), RANK ** -0.5, 0.375, ((0, 4),))
    coef_left = jnp.clip(jax.random.uniform(keys[4], (TERMS, 3, N), jnp.float32, -1.5, 1.5) * block_scale(keys[4], (TERMS, 3, N), ((0, 4),), -0.4, 0.0), -1.5, 1.5)
    coef_right = jnp.clip(jax.random.uniform(keys[5], (TERMS, 3, N), jnp.float32, -1.5, 1.5) * block_scale(keys[5], (TERMS, 3, N), ((0, 4),), -0.4, 0.0), -1.5, 1.5)
    projected = gaussian(keys[6], (N, SLAB, RANK, N), 1.0, 6.0, ((0, 4), (1, 2), (2, 4)))
    return {"core_left": core_left, "core_right": core_right, "env_left": env_left, "env_right": env_right, "coef_left": coef_left, "coef_right": coef_right, "projected": projected}


def stencil(field, coef):
    zero = jnp.zeros_like(field[..., :1])
    before = jnp.concatenate([zero, field[..., :-1]], axis=-1)
    after = jnp.concatenate([field[..., 1:], zero], axis=-1)
    return coef[0] * field + coef[1] * before + coef[2] * after


def reference(core_left, core_right, env_left, env_right, coef_left, coef_right, projected):
    left_wide = core_left.astype(jnp.float32)
    right_wide = core_right.astype(jnp.float32)

    def per_term(total, inputs):
        left_env, right_env, left_coef, right_coef = inputs
        left_field = stencil(left_wide, left_coef).astype(jnp.bfloat16)
        left_frame = jnp.einsum("pq,qrs->rps", left_env.astype(jnp.float32), left_field.astype(jnp.float32)).astype(jnp.bfloat16)
        right_field = stencil(right_wide, right_coef).astype(jnp.bfloat16)
        right_frame = jnp.einsum("bq,rqj->rbj", right_env.astype(jnp.float32), right_field.astype(jnp.float32)).astype(jnp.bfloat16)
        total = total + jnp.einsum("rai,rbj->jabi", left_frame.astype(jnp.float32), right_frame.astype(jnp.float32))
        return total, None

    start = jnp.zeros((N, SLAB, RANK, N), jnp.float32)
    total, unused = lax.scan(per_term, start, (env_left, env_right, coef_left, coef_right))
    return (projected.astype(jnp.float32) - total).astype(jnp.bfloat16)
```

```python
import functools

import jax
import jax.numpy as jnp
from jax import lax
from jax.experimental import pallas as pl
from jax.experimental.pallas import tpu as pltpu
from jax.sharding import PartitionSpec as P

MESH = pl.DeviceIdType.MESH
ANY = pl.BlockSpec(memory_space=pl.ANY)
VMEM = pl.BlockSpec(memory_space=pltpu.VMEM)
CHUNK = 16
BATCH = 8


def exchange_kernel(
    L, C, T, cr, er, el, cf, cl, crg, erg, lfg, cfg,
    elg, el_all, coef_rows, spread, lf, local_sem, cr_send, cr_recv, crp_send, crp_recv,
    lf_send, lf_recv, lfp_send, lfp_recv, z_send, z_recv,
):
    l, c, z = lax.axis_index("lrow"), lax.axis_index("rcol"), lax.axis_index("term")
    partner = c + 1 - 2 * lax.rem(c, 2)
    H = C // 2
    plane = [(dl, dc) for dl in range(L) for dc in range(H) if dl or dc]

    def at(dl, dc):
        return lax.rem(l + dl, L), lax.rem(c + 2 * dc, C)

    def source(dl, dc):
        return lax.rem(l + L - dl, L), lax.rem(c + C - 2 * dc, C)

    def send(src, dst, sems, recvs, k, where):
        copy = pltpu.make_async_remote_copy(
            src_ref=src, dst_ref=dst, send_sem=sems.at[k], recv_sem=recvs.at[k],
            device_id=where, device_id_type=MESH)
        copy.start()
        return copy

    barrier = pltpu.get_barrier_semaphore()
    for dl, dc in plane:
        pl_, pc = at(dl, dc)
        pl.semaphore_signal(barrier, inc=1, device_id={"lrow": pl_, "rcol": pc}, device_id_type=MESH)
    pl.semaphore_signal(barrier, inc=1, device_id={"rcol": partner}, device_id_type=MESH)
    for d in range(1, T):
        pl.semaphore_signal(barrier, inc=1, device_id={"term": lax.rem(z + d, T)}, device_id_type=MESH)
    pl.semaphore_wait(barrier, len(plane) + 1 + T - 1)

    small = []
    for d in range(1, T):
        where = {"term": lax.rem(z + d, T)}
        small.append(send(el, elg.at[z], z_send, z_recv, 3 * d, where))
        small.append(send(cf, cfg.at[z], z_send, z_recv, 3 * d + 1, where))
    own = [
        pltpu.make_async_copy(el, elg.at[z], local_sem.at[0]),
        pltpu.make_async_copy(cf, cfg.at[z], local_sem.at[1]),
        pltpu.make_async_copy(er, erg.at[z], local_sem.at[2]),
        pltpu.make_async_copy(cr, crg.at[:, l, c], local_sem.at[3]),
    ]
    for copy in own:
        copy.start()
    blocks = []
    for k, (dl, dc) in enumerate(plane):
        pl_, pc = at(dl, dc)
        blocks.append(send(cr, crg.at[:, l, c], cr_send, cr_recv, k, {"lrow": pl_, "rcol": pc}))
    to_partner = [send(cr, crg.at[:, l, c], crp_send, crp_recv, len(plane), {"rcol": partner})]
    envs = [send(er, erg.at[z], z_send, z_recv, 3 * d + 2, {"term": lax.rem(z + d, T)}) for d in range(1, T)]

    own[0].wait()
    own[1].wait()
    for copy in small:
        copy.wait()

    terms, slab = lf.shape[0] // T, lf.shape[2] // 128
    per = terms * slab
    lane = lax.broadcasted_iota(jnp.int32, (slab, 128), 1)
    for s in range(T):
        el_all[s * per:(s + 1) * per, :] = elg[s, 0:per, :]
        for t in range(terms):
            at_row = s * per + t * slab
            for k in range(3):
                row = jnp.broadcast_to(cfg[s, t * 6 + k:t * 6 + k + 1, :], (slab, 128))
                if k == 1:
                    row = jnp.where(lane == 0, 0.0, row)
                if k == 2:
                    row = jnp.where(lane == 127, 0.0, row)
                coef_rows[k, at_row:at_row + slab, :] = row
    for r0 in range(0, lf.shape[1], CHUNK):
        frame = jnp.dot(el_all[...].astype(jnp.bfloat16), cl[:, r0 * 128:(r0 + CHUNK) * 128],
                        preferred_element_type=jnp.float32)
        for r in range(CHUNK):
            x = frame[:, r * 128:(r + 1) * 128]
            spread[r] = (coef_rows[0] * x + coef_rows[1] * pltpu.roll(x, 1, 1)
                         + coef_rows[2] * pltpu.roll(x, 127, 1))
        for t in range(T * terms):
            for a in range(slab):
                lf[t, r0:r0 + CHUNK, a * 128:(a + 1) * 128] = spread[:, t * slab + a, :].astype(jnp.bfloat16)

    frames = []
    for dc in range(1, H):
        _, pc = at(0, dc)
        frames.append(send(lf, lfg.at[:, c], lf_send, lf_recv, dc - 1, {"rcol": pc}))
    frames_partner = [send(lf, lfg.at[:, c], lfp_send, lfp_recv, 0, {"rcol": partner})]
    own.append(pltpu.make_async_copy(lf, lfg.at[:, c], local_sem.at[4]))
    own[-1].start()

    for k, (dl, dc) in enumerate(plane):
        blocks[k].wait_recv()
        sl, sc = source(dl, dc)
        to_partner.append(send(crg.at[:, sl, sc], crg.at[:, sl, sc], crp_send, crp_recv, k, {"rcol": partner}))
    for dc in range(1, H):
        frames[dc - 1].wait_recv()
        _, sc = source(0, dc)
        frames_partner.append(send(lfg.at[:, sc], lfg.at[:, sc], lfp_send, lfp_recv, dc, {"rcol": partner}))
    for copy in envs + to_partner + frames_partner:
        copy.wait()
    for copy in blocks + frames:
        copy.wait_send()
    for copy in own[2:]:
        copy.wait()


def residual_kernel(coef, cr, er, lf, proj, out, h, rf):
    g = pl.program_id(0)
    batch, slab, bb = out.shape[0], out.shape[1], out.shape[2]
    rank = cr.shape[2]
    terms = er.shape[0] // bb
    for s in range(batch + 2):
        j = g * batch + s
        block = jnp.concatenate([cr[j, i] for i in range(cr.shape[1])], axis=1)
        h[s % 4] = lax.dot_general(er[...], block, (((1,), (1,)), ((), ())), preferred_element_type=jnp.float32)
        if s < 2:
            continue
        jj = s - 2
        for t in range(terms):
            rows = slice(t * bb, (t + 1) * bb)
            c = [coef[t * 3 + k, g * batch + jj] for k in range(3)]
            field = (c[0] * h[(jj + 1) % 4, rows, :] + c[1] * h[jj % 4, rows, :] + c[2] * h[(jj + 2) % 4, rows, :])
            rf[jj * bb:(jj + 1) * bb, t * rank:(t + 1) * rank] = field.astype(jnp.bfloat16)
    total = jnp.dot(rf[...], lf[...], preferred_element_type=jnp.float32)
    for jj in range(batch):
        for a in range(slab):
            part = total[jj * bb:(jj + 1) * bb, a * 128:(a + 1) * 128]
            out[jj, a] = (proj[jj, a].astype(jnp.float32) - part).astype(jnp.bfloat16)


def on_device(L, C, T, core_left, core_right, env_left, env_right, coef_left, coef_right, projected):
    terms, slab, rank = env_left.shape
    rb, qb, n = core_right.shape
    jb, _, bb, _ = projected.shape
    z, c = lax.axis_index("term"), lax.axis_index("rcol")
    cr = lax.dynamic_slice_in_dim(jnp.pad(core_right, ((0, 0), (0, 0), (1, 1))), z * jb, jb + 2, 2)
    cr = jnp.transpose(cr, (2, 0, 1))
    er = lax.dynamic_slice_in_dim(env_right, c * bb, bb, 1)
    pad = -(terms * slab) % 8
    el = jnp.pad(env_left.astype(jnp.float32).reshape(terms * slab, rank), ((0, pad), (0, 0)))
    cf = jnp.concatenate([coef_left, coef_right], axis=1).reshape(terms * 6, n)
    cf = jnp.pad(cf, ((0, -(terms * 6) % 8), (0, 0)))
    cl = core_left.reshape(rank, rb * n)
    plane = L * C // 2
    dma = pltpu.SemaphoreType.DMA
    bf16, f32 = jnp.bfloat16, jnp.float32
    crg, erg, lfg, cfg = pl.pallas_call(
        functools.partial(exchange_kernel, L, C, T),
        out_shape=(
            jax.ShapeDtypeStruct((jb + 2, L, C, rb, qb), bf16),
            jax.ShapeDtypeStruct((T, terms, bb, rank), bf16),
            jax.ShapeDtypeStruct((T * terms, C, rb, slab * n), bf16),
            jax.ShapeDtypeStruct((T,) + cf.shape, f32),
        ),
        in_specs=[ANY, ANY, VMEM, VMEM, VMEM],
        out_specs=(ANY, ANY, ANY, VMEM),
        scratch_shapes=[
            pltpu.VMEM((T,) + el.shape, f32),
            pltpu.VMEM((T * terms * slab, rank), f32),
            pltpu.VMEM((3, T * terms * slab, n), f32),
            pltpu.VMEM((CHUNK, T * terms * slab, n), f32),
            pltpu.VMEM((T * terms, rb, slab * n), bf16),
            dma((5,)),
            dma((plane,)), dma((plane,)), dma((plane,)), dma((plane,)),
            dma((C // 2,)), dma((C // 2,)), dma((C // 2,)), dma((C // 2,)),
            dma((3 * T,)), dma((3 * T,)),
        ],
        compiler_params=pltpu.CompilerParams(
            collective_id=0, has_side_effects=True, vmem_limit_bytes=40 * 2**20),
    )(cr, er, el, cf, cl)
    coef = cfg[:, :terms * 6].reshape(T * terms, 2, 3, n)[:, 1].reshape(T * terms * 3, n)
    coef = lax.dynamic_slice_in_dim(coef, z * jb, jb, 1)
    whole = lambda *shape: pl.BlockSpec(shape, lambda g: (0,) * len(shape))
    tile = pl.BlockSpec((BATCH, slab, bb, n), lambda g: (g, 0, 0, 0))
    return pl.pallas_call(
        residual_kernel,
        grid=(jb // BATCH,),
        out_shape=jax.ShapeDtypeStruct(projected.shape, bf16),
        in_specs=[
            pl.BlockSpec(memory_space=pltpu.SMEM),
            whole(jb + 2, L, rank, qb),
            whole(T * terms * bb, rank),
            whole(T * terms * rank, slab * n),
            tile,
        ],
        out_specs=tile,
        scratch_shapes=[
            pltpu.VMEM((4, T * terms * bb, rank), f32),
            pltpu.VMEM((BATCH * bb, T * terms * rank), bf16),
        ],
        compiler_params=pltpu.CompilerParams(vmem_limit_bytes=56 * 2**20),
    )(
        coef,
        crg.reshape(jb + 2, L, rank, qb),
        erg.reshape(T * terms * bb, rank),
        lfg.reshape(T * terms * rank, slab * n),
        projected,
    )


def solution(mesh):
    L, C, T = mesh.shape["lrow"], mesh.shape["rcol"], mesh.shape["term"]
    return jax.shard_map(
        functools.partial(on_device, L, C, T),
        mesh=mesh,
        in_specs=(
            P(None, "rcol", None),
            P("rcol", "lrow", None),
            P("term", "lrow", None),
            P("term", None, None),
            P("term", None, None),
            P("term", None, None),
            P("term", "lrow", "rcol", None),
        ),
        out_specs=P("term", "lrow", "rcol", None),
        check_vma=False,
    )
```

```python
import functools

import jax
import jax.numpy as jnp
from jax import lax
from jax.experimental import pallas as pl
from jax.experimental.pallas import tpu as pltpu
from jax.sharding import PartitionSpec as P

MESH = pl.DeviceIdType.MESH
VMEM = pl.BlockSpec(memory_space=pltpu.VMEM)
CHUNK = 16
BATCH = 8
PIECES = 5


def exchange_kernel(
    L, C, T, cr, er, el, cfl, cfr, cl, crg, erg, lfg, cfg,
    el_own, elg, clg, el_all, coef_rows, rows, spread, lf, local_sem, cr_send, cr_recv, crp_send, crp_recv,
    lf_send, lf_recv, lfz_send, lfz_recv, lfp_send, lfp_recv, z_send, z_recv,
):
    l, c, z = lax.axis_index("lrow"), lax.axis_index("rcol"), lax.axis_index("term")
    partner = {"rcol": c + 1 - 2 * lax.rem(c, 2)}
    parity = lax.rem(z, 2)
    beside = {"term": z + 1 - 2 * parity}
    H = C // 2
    terms, slab, _ = el.shape
    per = terms * slab

    def send(src, dst, sems, recvs, k, where):
        copy = pltpu.make_async_remote_copy(
            src_ref=src, dst_ref=dst, send_sem=sems.at[k], recv_sem=recvs.at[k],
            device_id=where, device_id_type=MESH)
        copy.start()
        return copy

    def row_peer(d):
        return {"lrow": lax.rem(l + d, L)}

    def col_peer(d):
        return {"rcol": lax.rem(c + 2 * d, C)}

    def term_peer(d):
        return {"term": lax.rem(z + d, T)}

    def row_source(d):
        return lax.rem(l + L - d, L)

    def col_source(d):
        return lax.rem(c + C - 2 * d, C)

    barrier = pltpu.get_barrier_semaphore()
    peers = ([row_peer(d) for d in range(1, L)] + [col_peer(d) for d in range(1, H)]
             + [term_peer(d) for d in range(1, T)] + [partner])
    for peer in peers:
        pl.semaphore_signal(barrier, inc=1, device_id=peer, device_id_type=MESH)
    el_own[0:per, :] = el[...].astype(jnp.float32).reshape(per, el.shape[2])
    pl.semaphore_wait(barrier, len(peers))

    small = []
    for d in range(1, T):
        small.append(send(el_own, elg.at[z], z_send, z_recv, 4 * d, term_peer(d)))
        small.append(send(cfl, clg.at[z], z_send, z_recv, 4 * d + 1, term_peer(d)))
    blocks = {}
    for d in range(1, H):
        blocks[0, d] = send(cr, crg.at[:, l, c], cr_send, cr_recv, d, col_peer(d))
    for d in range(1, L):
        blocks[d, 0] = send(cr, crg.at[:, l, c], cr_send, cr_recv, d * H, row_peer(d))
    sent = []
    for d in range(1, T):
        sent.append(send(cfr, cfg.at[z], z_send, z_recv, 4 * d + 2, term_peer(d)))
        sent.append(send(er, erg.at[z], z_send, z_recv, 4 * d + 3, term_peer(d)))
    sent.append(send(cr, crg.at[:, l, c], crp_send, crp_recv, 0, partner))
    own = [
        pltpu.make_async_copy(el_own, elg.at[z], local_sem.at[0]),
        pltpu.make_async_copy(cfl, clg.at[z], local_sem.at[1]),
        pltpu.make_async_copy(cfr, cfg.at[z], local_sem.at[2]),
        pltpu.make_async_copy(er, erg.at[z], local_sem.at[3]),
        pltpu.make_async_copy(cr, crg.at[:, l, c], local_sem.at[4]),
    ]
    for copy in own:
        copy.start()
    own[0].wait()
    own[1].wait()
    for copy in small:
        copy.wait()

    lane = lax.broadcasted_iota(jnp.int32, (slab, 128), 1)
    for s in range(T):
        el_all[s * per:(s + 1) * per, :] = elg[s, 0:per, :]
        for t in range(terms):
            at_row = s * per + t * slab
            for k in range(3):
                row = jnp.broadcast_to(clg[s, t, k:k + 1, :], (slab, 128))
                if k == 1:
                    row = jnp.where(lane == 0, 0.0, row)
                if k == 2:
                    row = jnp.where(lane == 127, 0.0, row)
                coef_rows[k, at_row:at_row + slab, :] = row

    @pl.loop(0, lf.shape[1] // CHUNK)
    def _(chunk):
        span = pl.ds(pl.multiple_of(chunk * CHUNK, CHUNK), CHUNK)
        rows[...] = cl[:, span, :].astype(jnp.float32)
        env = el_all[...].astype(jnp.bfloat16)
        for r in range(0, CHUNK, 2):
            block = jnp.concatenate([rows[:, r, :], rows[:, r + 1, :]], axis=1).astype(jnp.bfloat16)
            frame = jnp.dot(env, block, preferred_element_type=jnp.float32)
            for s in range(2):
                x = frame[:, s * 128:(s + 1) * 128]
                spread[r + s] = (coef_rows[0] * x + coef_rows[1] * pltpu.roll(x, 1, 1)
                                 + coef_rows[2] * pltpu.roll(x, 127, 1))
        for t in range(T * terms):
            for a in range(slab):
                lf[t, span, a * 128:(a + 1) * 128] = spread[:, t * slab + a, :].astype(jnp.bfloat16)

    step = T * terms // 2 // PIECES
    mine, theirs = parity * (T * terms // 2), (1 - parity) * (T * terms // 2)
    frames = {}
    for p in range(PIECES):
        for d in range(1, H):
            span = pl.ds(mine + p * step, step)
            frames[p, d] = send(lf.at[span], lfg.at[span, c], lf_send, lf_recv, p * H + d, col_peer(d))
    sent.append(send(lf, lfg.at[:, c], lfp_send, lfp_recv, 0, partner))
    own.append(pltpu.make_async_copy(lf, lfg.at[:, c], local_sem.at[5]))
    own[-1].start()

    for d in range(1, H):
        blocks[0, d].wait_recv()
        block = crg.at[:, l, col_source(d)]
        for e in range(1, L):
            blocks[e, d] = send(block, block, cr_send, cr_recv, e * H + d, row_peer(e))
        sent.append(send(block, block, crp_send, crp_recv, d, partner))
    for e in range(1, L):
        blocks[e, 0].wait_recv()
        block = crg.at[:, row_source(e), c]
        sent.append(send(block, block, crp_send, crp_recv, e * H, partner))
    onward = {}
    for p in range(PIECES):
        for d in range(1, H):
            frames[p, d].wait_recv()
            piece = lfg.at[pl.ds(mine + p * step, step), col_source(d)]
            onward[p, d] = send(piece, piece, lfz_send, lfz_recv, p * H + d, beside)
            sent.append(send(piece, piece, lfp_send, lfp_recv, p * H + d, partner))
    for e in range(1, L):
        for d in range(1, H):
            blocks[e, d].wait_recv()
            block = crg.at[:, row_source(e), col_source(d)]
            sent.append(send(block, block, crp_send, crp_recv, e * H + d, partner))
    for p in range(PIECES):
        for d in range(1, H):
            onward[p, d].wait_recv()
            piece = lfg.at[pl.ds(theirs + p * step, step), col_source(d)]
            sent.append(send(piece, piece, lfp_send, lfp_recv, (PIECES + p) * H + d, partner))
    for copy in sent:
        copy.wait()
    for copies in (blocks, frames, onward):
        for copy in copies.values():
            copy.wait_send()
    for copy in own[2:]:
        copy.wait()


def residual_kernel(proj_rows, coef, cr, er, lf, proj, out, h, rf):
    g = pl.program_id(0)
    batch, slab, bb = out.shape[0], out.shape[1], out.shape[2]
    rank = cr.shape[2]
    terms = er.shape[0] // bb
    first = lax.axis_index("term") * proj_rows
    for s in range(batch + 2):
        j = g * batch + s
        block = jnp.concatenate([cr[j, i] for i in range(cr.shape[1])], axis=1)
        h[s % 4] = lax.dot_general(er[...], block, (((1,), (1,)), ((), ())), preferred_element_type=jnp.float32)
        if s < 2:
            continue
        jj = s - 2
        for t in range(terms):
            rows = slice(t * bb, (t + 1) * bb)
            c = [coef[t * 3 + k, first + g * batch + jj] for k in range(3)]
            field = (c[0] * h[(jj + 1) % 4, rows, :] + c[1] * h[jj % 4, rows, :] + c[2] * h[(jj + 2) % 4, rows, :])
            rf[jj * bb:(jj + 1) * bb, t * rank:(t + 1) * rank] = field.astype(jnp.bfloat16)
    total = jnp.dot(rf[...], lf[...], preferred_element_type=jnp.float32)
    for jj in range(batch):
        for a in range(slab):
            part = total[jj * bb:(jj + 1) * bb, a * 128:(a + 1) * 128]
            out[jj, a] = (proj[jj, a].astype(jnp.float32) - part).astype(jnp.bfloat16)


def on_device(L, C, T, core_left, core_right, env_left, env_right, coef_left, coef_right, projected):
    terms, slab, rank = env_left.shape
    rb, qb, n = core_right.shape
    jb, _, bb, _ = projected.shape
    z, c = lax.axis_index("term"), lax.axis_index("rcol")
    cr = lax.dynamic_slice_in_dim(jnp.pad(core_right, ((0, 0), (0, 0), (1, 1))), z * jb, jb + 2, 2)
    cr = jnp.transpose(cr, (2, 0, 1))
    er = lax.dynamic_slice_in_dim(env_right, c * bb, bb, 1)
    plane = L * C // 2
    parts = PIECES * (C // 2)
    dma = pltpu.SemaphoreType.DMA
    bf16, f32 = jnp.bfloat16, jnp.float32
    crg, erg, lfg, cfg = pl.pallas_call(
        functools.partial(exchange_kernel, L, C, T),
        out_shape=(
            jax.ShapeDtypeStruct((jb + 2, L, C, rb, qb), bf16),
            jax.ShapeDtypeStruct((T, terms, bb, rank), bf16),
            jax.ShapeDtypeStruct((T * terms, C, rb, slab * n), bf16),
            jax.ShapeDtypeStruct((T, terms, 3, n), f32),
        ),
        in_specs=[VMEM] * 6,
        out_specs=(VMEM,) * 4,
        scratch_shapes=[
            pltpu.VMEM((-(-terms * slab // 8) * 8, rank), f32),
            pltpu.VMEM((T, -(-terms * slab // 8) * 8, rank), f32),
            pltpu.VMEM((T, terms, 3, n), f32),
            pltpu.VMEM((T * terms * slab, rank), f32),
            pltpu.VMEM((3, T * terms * slab, n), f32),
            pltpu.VMEM((rank, CHUNK, n), f32),
            pltpu.VMEM((CHUNK, T * terms * slab, n), f32),
            pltpu.VMEM((T * terms, rb, slab * n), bf16),
            dma((6,)),
            dma((plane,)), dma((plane,)), dma((plane,)), dma((plane,)),
            dma((parts,)), dma((parts,)), dma((parts,)), dma((parts,)), dma((2 * parts,)), dma((2 * parts,)),
            dma((4 * T,)), dma((4 * T,)),
        ],
        compiler_params=pltpu.CompilerParams(
            collective_id=0, has_side_effects=True, vmem_limit_bytes=30 * 2**20),
    )(cr, er, env_left, coef_left, coef_right, core_left)
    tile = pl.BlockSpec((BATCH, slab, bb, n), lambda g: (g, 0, 0, 0))
    return pl.pallas_call(
        functools.partial(residual_kernel, jb),
        grid=(jb // BATCH,),
        out_shape=jax.ShapeDtypeStruct(projected.shape, bf16),
        in_specs=[pl.BlockSpec(memory_space=pltpu.SMEM), VMEM, VMEM, VMEM, tile],
        out_specs=tile,
        scratch_shapes=[
            pltpu.VMEM((4, T * terms * bb, rank), f32),
            pltpu.VMEM((BATCH * bb, T * terms * rank), bf16),
        ],
        compiler_params=pltpu.CompilerParams(vmem_limit_bytes=30 * 2**20),
    )(
        cfg.reshape(T * terms * 3, n),
        crg.reshape(jb + 2, L, rank, qb),
        erg.reshape(T * terms * bb, rank),
        lfg.reshape(T * terms * rank, slab * n),
        projected,
    )


def solution(mesh):
    L, C, T = mesh.shape["lrow"], mesh.shape["rcol"], mesh.shape["term"]
    return jax.shard_map(
        functools.partial(on_device, L, C, T),
        mesh=mesh,
        in_specs=(
            P(None, "rcol", None),
            P("rcol", "lrow", None),
            P("term", "lrow", None),
            P("term", None, None),
            P("term", None, None),
            P("term", None, None),
            P("term", "lrow", "rcol", None),
        ),
        out_specs=P("term", "lrow", "rcol", None),
        check_vma=False,
    )
```

```python
import functools

import jax
import jax.numpy as jnp
from jax import lax
from jax.experimental import pallas as pl
from jax.experimental.pallas import tpu as pltpu
from jax.sharding import PartitionSpec as P

MESH = pl.DeviceIdType.MESH
VMEM = pl.BlockSpec(memory_space=pltpu.VMEM)
CHUNK = 16
BATCH = 8
PIECES = 5


def fused_kernel(
    L, C, T, cr, er, el, cfl, cfr, cl, proj, out, crg, erg, lfg, cfg, coef, h, rf,
    el_own, elg, clg, el_all, coef_rows, rows, spread, lf, local_sem, cr_send, cr_recv, crp_send, crp_recv,
    lf_send, lf_recv, lfz_send, lfz_recv, lfp_send, lfp_recv, z_send, z_recv,
):
    l, c, z = lax.axis_index("lrow"), lax.axis_index("rcol"), lax.axis_index("term")
    partner = {"rcol": c + 1 - 2 * lax.rem(c, 2)}
    parity = lax.rem(z, 2)
    beside = {"term": z + 1 - 2 * parity}
    H = C // 2
    terms, slab, _ = el.shape
    per = terms * slab

    def send(src, dst, sems, recvs, k, where):
        copy = pltpu.make_async_remote_copy(
            src_ref=src, dst_ref=dst, send_sem=sems.at[k], recv_sem=recvs.at[k],
            device_id=where, device_id_type=MESH)
        copy.start()
        return copy

    def row_peer(d):
        return {"lrow": lax.rem(l + d, L)}

    def col_peer(d):
        return {"rcol": lax.rem(c + 2 * d, C)}

    def term_peer(d):
        return {"term": lax.rem(z + d, T)}

    def row_source(d):
        return lax.rem(l + L - d, L)

    def col_source(d):
        return lax.rem(c + C - 2 * d, C)

    barrier = pltpu.get_barrier_semaphore()
    peers = ([row_peer(d) for d in range(1, L)] + [col_peer(d) for d in range(1, H)]
             + [term_peer(d) for d in range(1, T)] + [partner])
    for peer in peers:
        pl.semaphore_signal(barrier, inc=1, device_id=peer, device_id_type=MESH)
    el_own[0:per, :] = el[...].astype(jnp.float32).reshape(per, el.shape[2])
    pl.semaphore_wait(barrier, len(peers))

    small = []
    for d in range(1, T):
        small.append(send(el_own, elg.at[z], z_send, z_recv, 4 * d, term_peer(d)))
        small.append(send(cfl, clg.at[z], z_send, z_recv, 4 * d + 1, term_peer(d)))
    blocks = {}
    for d in range(1, H):
        blocks[0, d] = send(cr, crg.at[:, l, c], cr_send, cr_recv, d, col_peer(d))
    for d in range(1, L):
        blocks[d, 0] = send(cr, crg.at[:, l, c], cr_send, cr_recv, d * H, row_peer(d))
    sent, environments, to_partner = [], [], []
    for d in range(1, T):
        environments.append(send(cfr, cfg.at[z], z_send, z_recv, 4 * d + 2, term_peer(d)))
        environments.append(send(er, erg.at[z], z_send, z_recv, 4 * d + 3, term_peer(d)))
    to_partner.append(send(cr, crg.at[:, l, c], crp_send, crp_recv, 0, partner))
    own = [
        pltpu.make_async_copy(el_own, elg.at[z], local_sem.at[0]),
        pltpu.make_async_copy(cfl, clg.at[z], local_sem.at[1]),
        pltpu.make_async_copy(cfr, cfg.at[z], local_sem.at[2]),
        pltpu.make_async_copy(er, erg.at[z], local_sem.at[3]),
        pltpu.make_async_copy(cr, crg.at[:, l, c], local_sem.at[4]),
    ]
    for copy in own:
        copy.start()
    own[0].wait()
    own[1].wait()
    for copy in small:
        copy.wait()

    lane = lax.broadcasted_iota(jnp.int32, (slab, 128), 1)
    for s in range(T):
        el_all[s * per:(s + 1) * per, :] = elg[s, 0:per, :]
        for t in range(terms):
            at_row = s * per + t * slab
            for k in range(3):
                row = jnp.broadcast_to(clg[s, t, k:k + 1, :], (slab, 128))
                if k == 1:
                    row = jnp.where(lane == 0, 0.0, row)
                if k == 2:
                    row = jnp.where(lane == 127, 0.0, row)
                coef_rows[k, at_row:at_row + slab, :] = row

    @pl.loop(0, lf.shape[1] // CHUNK)
    def _(chunk):
        span = pl.ds(pl.multiple_of(chunk * CHUNK, CHUNK), CHUNK)
        rows[...] = cl[:, span, :].astype(jnp.float32)
        env = el_all[...].astype(jnp.bfloat16)
        for r in range(0, CHUNK, 2):
            block = jnp.concatenate([rows[:, r, :], rows[:, r + 1, :]], axis=1).astype(jnp.bfloat16)
            frame = jnp.dot(env, block, preferred_element_type=jnp.float32)
            for s in range(2):
                x = frame[:, s * 128:(s + 1) * 128]
                spread[r + s] = (coef_rows[0] * x + coef_rows[1] * pltpu.roll(x, 1, 1)
                                 + coef_rows[2] * pltpu.roll(x, 127, 1))
        for t in range(T * terms):
            for a in range(slab):
                lf[t, span, a * 128:(a + 1) * 128] = spread[:, t * slab + a, :].astype(jnp.bfloat16)

    step = T * terms // 2 // PIECES
    mine, theirs = parity * (T * terms // 2), (1 - parity) * (T * terms // 2)
    frames = {}
    for p in range(PIECES):
        for d in range(1, H):
            span = pl.ds(mine + p * step, step)
            frames[p, d] = send(lf.at[span], lfg.at[span, c], lf_send, lf_recv, p * H + d, col_peer(d))
    sent.append(send(lf, lfg.at[:, c], lfp_send, lfp_recv, 0, partner))
    own.append(pltpu.make_async_copy(lf, lfg.at[:, c], local_sem.at[5]))
    own[-1].start()

    for d in range(1, H):
        blocks[0, d].wait_recv()
        block = crg.at[:, l, col_source(d)]
        for e in range(1, L):
            blocks[e, d] = send(block, block, cr_send, cr_recv, e * H + d, row_peer(e))
        to_partner.append(send(block, block, crp_send, crp_recv, d, partner))
    for e in range(1, L):
        blocks[e, 0].wait_recv()
        block = crg.at[:, row_source(e), c]
        to_partner.append(send(block, block, crp_send, crp_recv, e * H, partner))
    onward = {}
    for p in range(PIECES):
        for d in range(1, H):
            frames[p, d].wait_recv()
            piece = lfg.at[pl.ds(mine + p * step, step), col_source(d)]
            onward[p, d] = send(piece, piece, lfz_send, lfz_recv, p * H + d, beside)
            sent.append(send(piece, piece, lfp_send, lfp_recv, p * H + d, partner))
    for e in range(1, L):
        for d in range(1, H):
            blocks[e, d].wait_recv()
            block = crg.at[:, row_source(e), col_source(d)]
            to_partner.append(send(block, block, crp_send, crp_recv, e * H + d, partner))
    for copy in environments + to_partner:
        copy.wait()
    for copy in own[2:5]:
        copy.wait()
    to_smem = pltpu.make_async_copy(cfg, coef, local_sem.at[6])
    to_smem.start()
    to_smem.wait()

    rank, bb = er.shape[2], er.shape[1]
    count = T * terms
    first = z * out.shape[0]

    @pl.loop(0, out.shape[0] // BATCH)
    def _(g):
        env = erg[...].reshape(count * bb, rank)
        for s in range(BATCH + 2):
            block = jnp.concatenate([crg[g * BATCH + s, i].reshape(rank, cr.shape[2]) for i in range(L)], axis=1)
            h[s % 4] = lax.dot_general(env, block, (((1,), (1,)), ((), ())), preferred_element_type=jnp.float32)
            if s < 2:
                continue
            jj = s - 2
            at_row = pl.multiple_of((g * BATCH + jj) * bb, bb)
            for t in range(count):
                span = slice(t * bb, (t + 1) * bb)
                k = [coef[t // terms, t % terms, i, first + g * BATCH + jj] for i in range(3)]
                field = k[0] * h[(jj + 1) % 4, span, :] + k[1] * h[jj % 4, span, :] + k[2] * h[(jj + 2) % 4, span, :]
                rf[pl.ds(at_row, bb), t * rank:(t + 1) * rank] = field.astype(jnp.bfloat16)

    for p in range(PIECES):
        for d in range(1, H):
            onward[p, d].wait_recv()
            piece = lfg.at[pl.ds(theirs + p * step, step), col_source(d)]
            sent.append(send(piece, piece, lfp_send, lfp_recv, (PIECES + p) * H + d, partner))
    for copy in sent:
        copy.wait()
    for copies in (blocks, frames, onward):
        for copy in copies.values():
            copy.wait_send()
    own[5].wait()

    @pl.loop(0, out.shape[0] // BATCH)
    def _(g):
        at_row = pl.multiple_of(g * BATCH * bb, BATCH * bb)
        total = jnp.dot(rf[pl.ds(at_row, BATCH * bb), :], lfg[...].reshape(count * rank, slab * 128),
                        preferred_element_type=jnp.float32)
        for jj in range(BATCH):
            for a in range(slab):
                part = total[jj * bb:(jj + 1) * bb, a * 128:(a + 1) * 128]
                j = g * BATCH + jj
                out[j, a] = (proj[j, a].astype(jnp.float32) - part).astype(jnp.bfloat16)


def on_device(L, C, T, core_left, core_right, env_left, env_right, coef_left, coef_right, projected):
    terms, slab, rank = env_left.shape
    rb, qb, n = core_right.shape
    jb, _, bb, _ = projected.shape
    z, c = lax.axis_index("term"), lax.axis_index("rcol")
    cr = lax.dynamic_slice_in_dim(jnp.pad(core_right, ((0, 0), (0, 0), (1, 1))), z * jb, jb + 2, 2)
    cr = jnp.transpose(cr, (2, 0, 1))
    er = lax.dynamic_slice_in_dim(env_right, c * bb, bb, 1)
    plane = L * C // 2
    parts = PIECES * (C // 2)
    dma = pltpu.SemaphoreType.DMA
    bf16, f32 = jnp.bfloat16, jnp.float32
    return pl.pallas_call(
        functools.partial(fused_kernel, L, C, T),
        out_shape=jax.ShapeDtypeStruct(projected.shape, bf16),
        in_specs=[VMEM] * 7,
        out_specs=VMEM,
        scratch_shapes=[
            pltpu.VMEM((jb + 2, L, C, rb, qb), bf16),
            pltpu.VMEM((T, terms, bb, rank), bf16),
            pltpu.VMEM((T * terms, C, rb, slab * n), bf16),
            pltpu.VMEM((T, terms, 3, n), f32),
            pltpu.SMEM((T, terms, 3, n), f32),
            pltpu.VMEM((4, T * terms * bb, rank), f32),
            pltpu.VMEM((jb * bb, T * terms * rank), bf16),
            pltpu.VMEM((-(-terms * slab // 8) * 8, rank), f32),
            pltpu.VMEM((T, -(-terms * slab // 8) * 8, rank), f32),
            pltpu.VMEM((T, terms, 3, n), f32),
            pltpu.VMEM((T * terms * slab, rank), f32),
            pltpu.VMEM((3, T * terms * slab, n), f32),
            pltpu.VMEM((rank, CHUNK, n), f32),
            pltpu.VMEM((CHUNK, T * terms * slab, n), f32),
            pltpu.VMEM((T * terms, rb, slab * n), bf16),
            dma((7,)),
            dma((plane,)), dma((plane,)), dma((plane,)), dma((plane,)),
            dma((parts,)), dma((parts,)), dma((parts,)), dma((parts,)), dma((2 * parts,)), dma((2 * parts,)),
            dma((4 * T,)), dma((4 * T,)),
        ],
        compiler_params=pltpu.CompilerParams(
            collective_id=0, has_side_effects=True, vmem_limit_bytes=60 * 2**20),
    )(cr, er, env_left, coef_left, coef_right, core_left, projected)


def solution(mesh):
    L, C, T = mesh.shape["lrow"], mesh.shape["rcol"], mesh.shape["term"]
    return jax.shard_map(
        functools.partial(on_device, L, C, T),
        mesh=mesh,
        in_specs=(
            P(None, "rcol", None),
            P("rcol", "lrow", None),
            P("term", "lrow", None),
            P("term", None, None),
            P("term", None, None),
            P("term", None, None),
            P("term", "lrow", "rcol", None),
        ),
        out_specs=P("term", "lrow", "rcol", None),
        check_vma=False,
    )
```
